512 devices in a mesh: space: 32 (over z, core), tm: 16 (over x, y).
Axes of the slice: x: 4, y: 4, z: 16, core: 2. Of those that a mesh axis runs over, the one named last changes fastest.
Arguments:
- recordings: bfloat16 [2, 3, 512, 32768], P(None, None, 'space', 'tm'), may hold values from -30 to 30
- owner: int32 [512, 1], P('space'), may hold values from 0 to 31; in each aligned block of 16 rows (0 to 15, 16 to 31, ...) at most 2 rows name the same one
- valid_range: int32 [512, 2], P('space'), may hold values from 0 to 32768, as said below
- bin_mask: int32 [512, 96], P('space'), may hold values 0 or 1
Outputs:
- adjoint: bfloat16 [3, 2048, 32768], P(None, 'space', 'tm')
The draws below stay inside these ranges and needn't reach their ends.
Inputs may be any that keep to these rules, and one draw needn't show every extreme that they name: `owner`: among the 16 receivers listed on one index of space, no subdomain owns more than 2; some subdomain owns exactly 2 of them. `valid_range`: column 0 is below column 1 in every row.
All inputs are finite; a program needn't handle non-finite values. No bound on the sum of `bin_mask` on one device may be relied on, other than what follows from the above.
Results may differ from the reference program's by a relative error of at most 0.013.
Values may be sent and summed in bfloat16 or wider, within the bound.
A program may use at most 128 MiB of HBM per device.

```python
import math
import jax
import jax.numpy as jnp
import numpy as np
from jax import lax

COMPONENTS = 3
BINS = 96
HOP = 256
HALO = 1024
REC_DEV = 16
SAMPLES_DEV = 2048
KERNEL = 2304
SAMPLES = 32768
RECEIVERS = 512
MOST = 2
SLOTS_DEV = 64
SLOTS = 2048
N_SPACE = 32


def draw_recordings(key, part):
    shape = (2, COMPONENTS, RECEIVERS, SAMPLES)
    keys = jax.random.split(key, 12)
    noise = jnp.clip(jax.random.normal(keys[0], shape, jnp.float32), -5.0, 5.0)
    low_env = 0.3
    high_env = 3.0
    times = jnp.arange(SAMPLES).astype(jnp.float32)
    signal = noise
    for wave in range(3):
        octaves = jax.random.uniform(keys[1 + wave], (2, COMPONENTS, RECEIVERS, 1), jnp.float32, 0.0, 7.0)
        freq = 0.25 * jnp.exp2(-octaves)
        amplitude = jnp.exp(jax.random.uniform(keys[4 + wave], (2, COMPONENTS, RECEIVERS, 1), jnp.float32, math.log(0.3), math.log(1.5)))
        offset = jax.random.uniform(keys[7 + wave], (2, COMPONENTS, RECEIVERS, 1), jnp.float32, 0.0, 1.0)
        cycles = freq * times[None, None, None, :] + offset
        phase = cycles - jnp.floor(cycles)
        signal = signal + amplitude * jnp.sin(2.0 * math.pi * phase)
    piece_len = SAMPLES_DEV // 2
    pieces = SAMPLES // piece_len
    envelope = jnp.exp(jax.random.uniform(keys[10], (2, COMPONENTS, RECEIVERS, pieces, 1), jnp.float32, math.log(low_env), math.log(high_env)))
    signal = (signal.reshape(2, COMPONENTS, RECEIVERS, pieces, piece_len) * envelope).reshape(shape)
    return signal.astype(jnp.bfloat16)


def draw_valid_range(key, part):
    first_key, last_key = jax.random.split(key)
    start = jax.random.randint(first_key, (RECEIVERS, 1), 0, SAMPLES // 3)
    end = jax.random.randint(last_key, (RECEIVERS, 1), 2 * SAMPLES // 3, SAMPLES + 1)
    start = start.at[0, 0].set(0)
    end = end.at[0, 0].set(SAMPLES)
    return jnp.concatenate([start, end], axis=1).astype(jnp.int32)


def plant(drawn, key, low, high):
    longest = drawn.shape.index(max(drawn.shape))
    spots = []
    for shift in (0, 1):
        where = [jax.random.randint(jax.random.fold_in(key, axis), (), 0, length) for axis, length in enumerate(drawn.shape)]
        where[longest] = (where[longest] + shift) % drawn.shape[longest]
        spots.append(tuple(where))
    return drawn.at[spots[0]].set(low).at[spots[1]].set(high)


def deal_out(key, own, number, rows, amount, top, most, slope):
    ranking = jax.random.permutation(key, amount)
    heavy_load, ordinary = shares(amount, rows * top, most, slope, True), shares(amount, rows * top, most, slope, False)
    places = jnp.arange(amount)

    def named(tallies, offset_by):
        used = int((tallies > 0).sum())
        fixed = max(1, used // 4)
        moved = fixed + (places - fixed + offset_by * (used - fixed)) % max(1, amount - fixed)
        return jnp.zeros((amount,), jnp.int32).at[ranking[jnp.where(places < fixed, places, moved)]].set(jnp.asarray(tallies, jnp.int32))

    tallies = jnp.where(number % 4 == 0, named(heavy_load, number // 4), named(ordinary, number - number // 4 - 1))
    mixed = jax.random.permutation(jax.random.fold_in(own, 3), amount)
    source_of, sink = mixed[0:amount // 2 * 2:2], mixed[1:amount // 2 * 2:2]
    room = jnp.minimum(tallies[source_of] - 1, most - tallies[sink]) // 2
    room = jnp.where((source_of == ranking[0]) | (sink == ranking[0]) | (tallies[sink] == 0), 0, jnp.maximum(room, 0))
    moved = jax.random.randint(jax.random.fold_in(own, 4), (amount // 2,), 0, 1 << 20) % (room + 1)
    tallies = tallies.at[source_of].add(-moved).at[sink].add(moved)
    items = jnp.searchsorted(jnp.cumsum(tallies), jnp.arange(rows * top), side="right").astype(jnp.int32)
    listing = items.reshape(top, rows).T
    listing = listing[jax.random.permutation(jax.random.fold_in(own, 1), rows)]
    offset_by = jax.random.randint(jax.random.fold_in(own, 2), (rows, 1), 0, top)
    return jnp.take_along_axis(listing, (jnp.arange(top)[None, :] + offset_by) % top, axis=1)


def shares(number_of, total, limit, lean, full):
    portions = [(1 << 20) // math.isqrt(standing ** lean) + 1 for standing in range(1, number_of + 1)]
    largest = limit if full else min(limit, max(-(-total // number_of), total * portions[0] // sum(portions)))
    least = 1 if total - largest >= number_of - 1 else 0
    given, rest = [largest] + [least] * (number_of - 1), total - largest - least * (number_of - 1)
    while rest > 0:
        movable = [i for i in range(1, number_of) if given[i] < largest] or [i for i in range(1, number_of) if given[i] < limit]
        whole, budget = sum([portions[i] for i in movable]), rest
        for i in movable:
            more = min(limit - given[i], max(1, budget * portions[i] // whole), rest)
            given[i] = given[i] + more
            rest = rest - more
    return np.array(given)


def setup_inputs(seed: int = 0) -> dict:
    key_list = jax.random.split(jax.random.key(seed), 5)
    recordings = draw_recordings(jax.random.fold_in(key_list[4], 71), 0)
    owner_keys = jax.random.split(jax.random.fold_in(key_list[1], 1), RECEIVERS // REC_DEV)
    owner_turns = jax.random.permutation(jax.random.fold_in(key_list[1], 3), RECEIVERS // REC_DEV)
    owner = jax.vmap(lambda own, number: deal_out(jax.random.fold_in(key_list[1], 2), own, number, REC_DEV, N_SPACE, 1, MOST, 2))(owner_keys, owner_turns).reshape((RECEIVERS, 1))
    valid_range = draw_valid_range(jax.random.fold_in(key_list[4], 71), 0)
    bin_mask = plant((jax.random.randint(key_list[3], (RECEIVERS, BINS), 0, 4) < 3).astype(jnp.int32), jax.random.fold_in(key_list[3], 1), 0, 1)
    return dict(recordings=recordings, owner=owner, valid_range=valid_range, bin_mask=bin_mask)


WATER = 0.1
EPSILON = 1e-06

def cq_kernel(kern_len, bins):
    octave_bins = bins // 8
    index = jnp.arange(bins).astype(jnp.float32)
    freq = 0.25 * jnp.exp2((index - (bins - 1)) / octave_bins)
    quality = 1.0 / (2.0 ** (1.0 / octave_bins) - 1.0)
    support = jnp.minimum(quality / freq, float(kern_len))
    offset = jnp.arange(kern_len).astype(jnp.float32) - 0.5 * (kern_len - 1)
    ratio = offset[:, None] / support[None, :]
    window = jnp.where(jnp.abs(ratio) < 0.5, 0.5 + 0.5 * jnp.cos(2.0 * math.pi * ratio), 0.0)
    window = window / jnp.sqrt(lax.optimization_barrier(jnp.sum(window * window, axis=0, keepdims=True)))
    cycles = offset[:, None] * freq[None, :]
    phase = cycles - jnp.floor(cycles)
    table = jnp.concatenate([window * jnp.cos(2.0 * math.pi * phase), -window * jnp.sin(2.0 * math.pi * phase)], axis=1)
    return table.astype(jnp.bfloat16)

def adjoint_of(syn_re, syn_im, obs_re, obs_im, weight):
    level = WATER * lax.optimization_barrier(jnp.mean(obs_re * obs_re + obs_im * obs_im, axis=(-2, -1), keepdims=True)) + EPSILON
    syn_norm = jnp.sqrt(syn_re * syn_re + syn_im * syn_im + level)
    obs_norm = jnp.sqrt(obs_re * obs_re + obs_im * obs_im + level)
    diff_re = weight * (syn_re / syn_norm - obs_re / obs_norm)
    diff_im = weight * (syn_im / syn_norm - obs_im / obs_norm)
    inner = (syn_re * diff_re + syn_im * diff_im) / (syn_norm * syn_norm * syn_norm)
    return (diff_re / syn_norm - syn_re * inner, diff_im / syn_norm - syn_im * inner)

def analyse(blocks, table, frames):
    taps = table.shape[0] // HOP
    unfolded = jnp.concatenate([blocks[..., tap:tap + frames, :] for tap in range(taps)], axis=-1)
    return jnp.einsum('...fh,hk->...fk', unfolded, table, precision=lax.Precision.HIGHEST)

def synthesise(coefs, table, frames):
    taps = table.shape[0] // HOP
    term = jnp.einsum('...fk,hk->...fh', coefs, table, precision=lax.Precision.HIGHEST)
    term = term.reshape(term.shape[:-1] + (taps, HOP))
    lead = len(term.shape) - 3
    ext = jnp.zeros(coefs.shape[:-2] + (frames + taps - 1, HOP), jnp.float32)
    for tap in range(taps):
        widths = [(0, 0)] * lead + [(tap, taps - 1 - tap), (0, 0)]
        ext = ext + jnp.pad(term[..., tap, :], widths)
    return ext

def reference(recordings, owner, valid_range, bin_mask):
    table = cq_kernel(KERNEL, BINS).astype(jnp.float32)
    frames_all = SAMPLES // HOP
    margin = HALO // HOP
    centers = jnp.arange(frames_all).astype(jnp.int32) * HOP + HOP // 2

    def one_block(block):
        start = (block * REC_DEV).astype(jnp.int32)
        traces = lax.dynamic_slice_in_dim(recordings, start, REC_DEV, 2).astype(jnp.float32)
        ranges = lax.dynamic_slice_in_dim(valid_range, start, REC_DEV, 0)
        masks = lax.dynamic_slice_in_dim(bin_mask, start, REC_DEV, 0)
        padded = jnp.pad(traces, ((0, 0), (0, 0), (0, 0), (HALO, HALO)))
        blocks = padded.reshape(2, COMPONENTS, REC_DEV, frames_all + 2 * margin, HOP)
        coefs = analyse(blocks, table, frames_all)
        coefs = lax.optimization_barrier(coefs.astype(jnp.bfloat16)).astype(jnp.float32)
        inside = (ranges[:, 0:1] <= centers[None, :]) & (centers[None, :] < ranges[:, 1:2])
        weight = inside.astype(jnp.float32)[:, :, None] * masks.astype(jnp.float32)[:, None, :]
        adj_re, adj_im = adjoint_of(coefs[0, ..., :BINS], coefs[0, ..., BINS:], coefs[1, ..., :BINS], coefs[1, ..., BINS:], weight)
        joined = jnp.concatenate([adj_re, adj_im], axis=-1)
        joined = lax.optimization_barrier(joined.astype(jnp.bfloat16)).astype(jnp.float32)
        ext = synthesise(joined, table, frames_all)
        series = ext[:, :, margin:margin + frames_all, :].reshape(COMPONENTS, REC_DEV, SAMPLES)
        return series.astype(jnp.bfloat16)
    mapped = lax.map(one_block, jnp.arange(N_SPACE).astype(jnp.int32))
    series_all = jnp.moveaxis(mapped, 0, 1).reshape(COMPONENTS, RECEIVERS, SAMPLES)
    target = owner[:, 0]
    onehot = (target[:, None] == jnp.arange(N_SPACE).astype(jnp.int32)[None, :]).astype(jnp.int32)
    onehot = onehot.reshape(N_SPACE, REC_DEV, N_SPACE)
    before = jnp.cumsum(onehot, axis=1) - onehot
    rank = lax.optimization_barrier(jnp.sum(before * onehot, axis=2)).reshape(RECEIVERS)
    source = jnp.arange(RECEIVERS).astype(jnp.int32) // REC_DEV
    slot = (target * SLOTS_DEV + source * MOST + rank).astype(jnp.int32)
    adjoint = jnp.zeros((COMPONENTS, SLOTS, SAMPLES), jnp.bfloat16).at[:, slot, :].set(series_all)
    return adjoint
```

```python
import math

import jax
import jax.numpy as jnp
from jax import lax
from jax.sharding import PartitionSpec as P

BINS = 96
HOP = 256
HALO = 1024
KERNEL = 2304


WATER = 0.1
EPSILON = 1e-06


def with_halo(block, sides, width):
    for axis, dim in sides:
        count = lax.axis_size(axis)
        forward = [(i, i + 1) for i in range(count - 1)]
        backward = [(target, source) for source, target in forward]
        low = lax.ppermute(
            lax.slice_in_dim(block, block.shape[dim] - width, None, axis=dim), axis, forward
        )
        high = lax.ppermute(lax.slice_in_dim(block, 0, width, axis=dim), axis, backward)
        block = jnp.concatenate([low, block, high], axis=dim)
    return block


def shifted(block, axis, distance):
    devices = range(lax.axis_size(axis))
    route = [(i - distance, i) for i in devices if i - distance in devices]
    return lax.ppermute(block, axis, route)


def cq_kernel(kern_len, bins):
    octave_bins = bins // 8
    index = jnp.arange(bins).astype(jnp.float32)
    freq = 0.25 * jnp.exp2((index - (bins - 1)) / octave_bins)
    quality = 1.0 / (2.0 ** (1.0 / octave_bins) - 1.0)
    support = jnp.minimum(quality / freq, float(kern_len))
    offset = jnp.arange(kern_len).astype(jnp.float32) - 0.5 * (kern_len - 1)
    ratio = offset[:, None] / support[None, :]
    window = jnp.where(jnp.abs(ratio) < 0.5, 0.5 + 0.5 * jnp.cos(2.0 * math.pi * ratio), 0.0)
    window = window / jnp.sqrt(jnp.sum(window * window, axis=0, keepdims=True))
    cycles = offset[:, None] * freq[None, :]
    phase = cycles - jnp.floor(cycles)
    table = jnp.concatenate(
        [window * jnp.cos(2.0 * math.pi * phase), -window * jnp.sin(2.0 * math.pi * phase)], axis=1
    )
    return table.astype(jnp.bfloat16)


def adjoint_of(syn_re, syn_im, obs_re, obs_im, weight):
    level = (
        WATER * jnp.mean(obs_re * obs_re + obs_im * obs_im, axis=(-2, -1), keepdims=True) + EPSILON
    )
    syn_norm = jnp.sqrt(syn_re * syn_re + syn_im * syn_im + level)
    obs_norm = jnp.sqrt(obs_re * obs_re + obs_im * obs_im + level)
    diff_re = weight * (syn_re / syn_norm - obs_re / obs_norm)
    diff_im = weight * (syn_im / syn_norm - obs_im / obs_norm)
    inner = (syn_re * diff_re + syn_im * diff_im) / (syn_norm * syn_norm * syn_norm)
    return (diff_re / syn_norm - syn_re * inner, diff_im / syn_norm - syn_im * inner)


def analyse(blocks, table, frames):
    taps = table.shape[0] // HOP
    unfolded = jnp.concatenate([blocks[..., tap : tap + frames, :] for tap in range(taps)], axis=-1)
    return jnp.einsum("...fh,hk->...fk", unfolded, table, preferred_element_type=jnp.float32)


def synthesise(coefs, table, frames):
    taps = table.shape[0] // HOP
    term = jnp.einsum("...fk,hk->...fh", coefs, table, preferred_element_type=jnp.float32)
    term = term.reshape(term.shape[:-1] + (taps, HOP))
    lead = len(term.shape) - 3
    ext = jnp.zeros(coefs.shape[:-2] + (frames + taps - 1, HOP), jnp.float32)
    for tap in range(taps):
        widths = [(0, 0)] * lead + [(tap, taps - 1 - tap), (0, 0)]
        ext = ext + jnp.pad(term[..., tap, :], widths)
    return ext


def frame_weight(ranges, masks, frames_all):
    centers = jnp.arange(frames_all, dtype=jnp.int32) * HOP + HOP // 2
    inside = (ranges[:, 0:1] <= centers[None, :]) & (centers[None, :] < ranges[:, 1:2])
    return inside.astype(jnp.float32)[:, :, None] * masks.astype(jnp.float32)[:, None, :]


def misfit(coefs, weight):
    adj_re, adj_im = adjoint_of(
        coefs[0, ..., :BINS],
        coefs[0, ..., BINS:],
        coefs[1, ..., :BINS],
        coefs[1, ..., BINS:],
        weight,
    )
    joined = jnp.concatenate([adj_re, adj_im], axis=-1)
    return joined.reshape(joined.shape[:2] + (joined.shape[2] * joined.shape[3],)).astype(
        jnp.bfloat16
    )


def on_device(recordings, owner, valid_range, bin_mask):
    table = cq_kernel(KERNEL, BINS)
    margin = HALO // HOP
    width = 2 * BINS
    groups = lax.axis_size("tm")
    comps = recordings.shape[1]
    rec_dev = recordings.shape[2]
    samples_dev = recordings.shape[3]
    frames_dev = samples_dev // HOP
    rec_group = rec_dev // groups
    first_row = lax.axis_index("tm") * rec_group
    ranges = lax.dynamic_slice_in_dim(valid_range, first_row, rec_group, 0)
    masks = lax.dynamic_slice_in_dim(bin_mask, first_row, rec_group, 0)
    extended = with_halo(recordings, (("tm", 3),), HALO)
    blocks = extended.reshape(2, comps, rec_dev, frames_dev + 2 * margin, HOP)
    coefs = analyse(blocks, table, frames_dev)
    packed = coefs.astype(jnp.bfloat16).reshape(2, comps, rec_dev, frames_dev * width)
    weight = frame_weight(ranges, masks, frames_dev * groups)
    pieces = lax.all_to_all(packed, "tm", split_axis=2, concat_axis=3, tiled=True)
    items = pieces.shape[1]
    frames_all = pieces.shape[3] // width
    local_coefs = pieces.astype(jnp.float32).reshape(2, items, rec_group, frames_all, width)
    adjoint_local = misfit(local_coefs, weight)
    adjoint_back = lax.all_to_all(adjoint_local, "tm", split_axis=2, concat_axis=1, tiled=True)
    adjoint_frames = adjoint_back.reshape(comps, rec_dev, frames_dev, width)
    ext = synthesise(adjoint_frames, table, frames_dev)
    flat = ext.reshape(comps, rec_dev, (frames_dev + 2 * margin) * HOP)
    middle = flat[:, :, HALO : HALO + samples_dev]
    from_before = shifted(flat[:, :, HALO + samples_dev :].astype(jnp.bfloat16), "tm", 1).astype(
        jnp.float32
    )
    from_after = shifted(flat[:, :, :HALO].astype(jnp.bfloat16), "tm", -1).astype(jnp.float32)
    middle = middle.at[:, :, :HALO].add(from_before)
    middle = middle.at[:, :, samples_dev - HALO :].add(from_after)
    series = middle.astype(jnp.bfloat16)
    count = lax.axis_size("space")
    most = max(2, 3 * rec_dev // (2 * count))
    target = owner[:, 0]
    place = jnp.arange(rec_dev, dtype=jnp.int32)
    earlier = (target[:, None] == target[None, :]) & (place[None, :] < place[:, None])
    rank = jnp.sum(earlier.astype(jnp.int32), axis=1)
    slot = target * most + rank
    select = (jnp.arange(count * most, dtype=jnp.int32)[:, None] == slot[None, :]).astype(
        jnp.bfloat16
    )
    outgoing = jnp.einsum("sr,crt->cst", select, series, preferred_element_type=jnp.float32).astype(
        jnp.bfloat16
    )
    return lax.all_to_all(outgoing, "space", split_axis=1, concat_axis=1, tiled=True)


def solution(mesh):
    return jax.shard_map(
        on_device,
        mesh=mesh,
        in_specs=(
            P(None, None, "space", "tm"),
            P("space", None),
            P("space", None),
            P("space", None),
        ),
        out_specs=P(None, "space", "tm"),
        check_vma=False,
    )
```

```python
import math

import jax
import jax.numpy as jnp
import ml_dtypes
import numpy as np
from jax import lax
from jax.sharding import PartitionSpec as P

BINS = 96
HOP = 256
HALO = 1024
KERNEL = 2304
TAPS = KERNEL // HOP
WATER = 0.1
EPSILON = 1e-06


def cq_table():
    f32 = np.float32
    octave_bins = BINS // 8
    index = np.arange(BINS).astype(f32)
    freq = f32(0.25) * np.exp2(((index - f32(BINS - 1)) / f32(octave_bins)).astype(np.float64)).astype(f32)
    quality = f32(1.0 / (2.0 ** (1.0 / octave_bins) - 1.0))
    support = np.minimum(quality / freq, f32(KERNEL))
    offset = np.arange(KERNEL).astype(f32) - f32(0.5 * (KERNEL - 1))
    ratio = (offset[:, None] / support[None, :]).astype(np.float64)
    window = np.where(np.abs(ratio) < 0.5, 0.5 + 0.5 * np.cos(2.0 * math.pi * ratio), 0.0)
    window = window / np.sqrt(np.sum(window * window, axis=0, keepdims=True))
    cycles = offset[:, None] * freq[None, :]
    phase = (cycles - np.floor(cycles)).astype(np.float64)
    table = np.concatenate(
        [window * np.cos(2.0 * math.pi * phase), -window * np.sin(2.0 * math.pi * phase)], axis=1
    )
    return table.astype(f32).astype(ml_dtypes.bfloat16)


def shifted(block, distance):
    count = lax.axis_size("tm")
    route = [(i - distance, i) for i in range(count) if 0 <= i - distance < count]
    return lax.ppermute(block, "tm", route)


def on_device(recordings, owner, valid_range, bin_mask):
    table = jnp.asarray(cq_table())
    margin = HALO // HOP
    comps, rec_dev, samples_dev = recordings.shape[1:]
    frames = samples_dev // HOP
    rows = comps * rec_dev
    blocks = recordings.reshape(2, rows, frames, HOP).transpose(0, 2, 1, 3)
    low = shifted(blocks[:, frames - margin :], 1)
    high = shifted(blocks[:, :margin], -1)
    ext = jnp.concatenate([low, blocks, high], axis=1)
    unfolded = jnp.concatenate([ext[:, tap : tap + frames] for tap in range(TAPS)], axis=-1)
    coefs = jnp.einsum("sfrh,hk->sfrk", unfolded, table, preferred_element_type=jnp.float32)
    coefs = coefs.astype(jnp.bfloat16).astype(jnp.float32)
    obs = coefs[1]
    frames_all = frames * lax.axis_size("tm")
    power = lax.psum(jnp.sum(obs * obs, axis=(0, 2)), "tm")
    level = (WATER * (power / (frames_all * BINS)) + EPSILON)[None, :, None]
    first = lax.axis_index("tm") * frames
    centers = (first + jnp.arange(frames, dtype=jnp.int32)) * HOP + HOP // 2
    inside = (valid_range[None, :, 0] <= centers[:, None]) & (centers[:, None] < valid_range[None, :, 1])
    weight = inside.astype(jnp.float32)[:, :, None] * bin_mask.astype(jnp.float32)[None]
    weight = jnp.tile(weight, (1, comps, 1))
    x_re, x_im = coefs[0, ..., :BINS], coefs[0, ..., BINS:]
    y_re, y_im = obs[..., :BINS], obs[..., BINS:]
    x_norm = jnp.sqrt(x_re * x_re + x_im * x_im + level)
    y_norm = jnp.sqrt(y_re * y_re + y_im * y_im + level)
    d_re = weight * (x_re / x_norm - y_re / y_norm)
    d_im = weight * (x_im / x_norm - y_im / y_norm)
    inner = (x_re * d_re + x_im * d_im) / (x_norm * x_norm * x_norm)
    adjoint = jnp.concatenate([d_re / x_norm - x_re * inner, d_im / x_norm - x_im * inner], axis=-1)
    adjoint = adjoint.astype(jnp.bfloat16)
    term = jnp.einsum("frk,hk->frh", adjoint, table, preferred_element_type=jnp.float32)
    flat = sum(
        jnp.pad(term[..., tap * HOP : (tap + 1) * HOP], ((tap, TAPS - 1 - tap), (0, 0), (0, 0)))
        for tap in range(TAPS)
    )
    middle = flat[margin : margin + frames]
    before = shifted(flat[margin + frames :].astype(jnp.bfloat16), 1).astype(jnp.float32)
    after = shifted(flat[:margin].astype(jnp.bfloat16), -1).astype(jnp.float32)
    middle = middle + jnp.concatenate([before, after], axis=0)
    series = middle.astype(jnp.bfloat16).reshape(frames, comps, rec_dev, HOP)
    count = lax.axis_size("space")
    most = max(2, 3 * rec_dev // (2 * count))
    target = owner[:, 0]
    place = jnp.arange(rec_dev, dtype=jnp.int32)
    earlier = (target[:, None] == target[None, :]) & (place[None, :] < place[:, None])
    slot = target * most + jnp.sum(earlier.astype(jnp.int32), axis=1)
    select = (jnp.arange(count * most, dtype=jnp.int32)[:, None] == slot[None, :]).astype(jnp.bfloat16)
    outgoing = jnp.einsum("sr,fcrh->cfsh", select, series, preferred_element_type=jnp.float32)
    outgoing = outgoing.astype(jnp.bfloat16).transpose(0, 2, 1, 3).reshape(comps, count * most, samples_dev)
    return lax.all_to_all(outgoing, "space", split_axis=1, concat_axis=1, tiled=True)


def solution(mesh):
    return jax.shard_map(
        on_device,
        mesh=mesh,
        in_specs=(
            P(None, None, "space", "tm"),
            P("space", None),
            P("space", None),
            P("space", None),
        ),
        out_specs=P(None, "space", "tm"),
        check_vma=False,
    )
```

```python
import functools
import math

import jax
import jax.numpy as jnp
import ml_dtypes
import numpy as np
from jax import lax
from jax.experimental import pallas as pl
from jax.experimental.pallas import tpu as pltpu
from jax.sharding import PartitionSpec as P

BINS = 96
HOP = 256
HALO = 1024
KERNEL = 2304
TAPS = KERNEL // HOP
MARGIN = HALO // HOP
WATER = 0.1
EPSILON = 1e-06
MOST = 2
LANES = 128
MESH = pl.DeviceIdType.MESH


def cq_table():
    f32 = np.float32
    octave_bins = BINS // 8
    index = np.arange(BINS).astype(f32)
    freq = f32(0.25) * np.exp2(((index - f32(BINS - 1)) / f32(octave_bins)).astype(np.float64)).astype(f32)
    quality = f32(1.0 / (2.0 ** (1.0 / octave_bins) - 1.0))
    support = np.minimum(quality / freq, f32(KERNEL))
    offset = np.arange(KERNEL).astype(f32) - f32(0.5 * (KERNEL - 1))
    ratio = (offset[:, None] / support[None, :]).astype(np.float64)
    window = np.where(np.abs(ratio) < 0.5, 0.5 + 0.5 * np.cos(2.0 * math.pi * ratio), 0.0)
    window = window / np.sqrt(np.sum(window * window, axis=0, keepdims=True))
    cycles = offset[:, None] * freq[None, :]
    phase = (cycles - np.floor(cycles)).astype(np.float64)
    table = np.zeros((KERNEL, 2 * LANES))
    table[:, :BINS] = window * np.cos(2.0 * math.pi * phase)
    table[:, LANES : LANES + BINS] = -window * np.sin(2.0 * math.pi * phase)
    return table.astype(f32).astype(ml_dtypes.bfloat16)


def ring_rows(chips, rec_dev):
    half = chips // 2
    return [min(rec_dev, 2 * MOST * (half - k) + MOST) for k in range(1, half + 1)]


def kernel(
    sizes, rec_in, owner, valid, mask, table_in, out, rec, table, bins, across,
    ext, coef, adj, acc, lv_out, lv_in, meta_out, meta_in, order, meta_s, order_s,
    edge_out, edge_in, flat, rows, packet, mate_out, mate_in, slots,
    halo_send, halo_recv, one_send, one_recv, edge_send, edge_recv, ring_send, ring_recv, mate_recv, local, *bufs,
):
    chips, groups, comps, rec_dev, frames = sizes
    half = chips // 2
    traces = comps * rec_dev
    per_row = frames * HOP // LANES
    hops = ring_rows(chips, rec_dev)
    f32, i32 = jnp.float32, jnp.int32

    space, t = lax.axis_index("space"), lax.axis_index("tm")
    z, core = space // 2, space % 2

    def band(d):
        return {"tm": lax.rem(t + d + groups, groups)}

    def chip(d):
        return {"space": lax.rem(z + d + chips, chips) * 2 + core}

    mate = {"space": z * 2 + 1 - core}

    def send(src, dst, ss, rs, to):
        copy = pltpu.make_async_remote_copy(src, dst, ss, rs, device_id=to, device_id_type=MESH)
        copy.start()
        return copy

    def wait_bytes(ref, sem):
        pltpu.make_async_copy(ref, ref, sem).wait()

    barrier = pltpu.get_barrier_semaphore()
    others = [band(d) for d in range(1, groups)] + [chip(d) for d in range(1, chips)] + [mate]
    for to in others:
        pl.semaphore_signal(barrier, inc=1, device_id=to, device_id_type=MESH)

    rec_copy = pltpu.make_async_copy(rec_in, rec, local.at[3])
    rec_copy.start()
    table_copy = pltpu.make_async_copy(table_in, table, local.at[4])
    table_copy.start()

    lane = lax.broadcasted_iota(i32, (rec_dev, LANES), 1)
    line = lax.broadcasted_iota(i32, (rec_dev, LANES), 0)
    listed = lane < rec_dev

    def widened(ref, n):
        across[n : n + 1, pl.ds(0, rec_dev)] = ref[n : n + 1, :]
        return jnp.broadcast_to(across[n : n + 1, :], (rec_dev, LANES))

    def upright(values):
        return jnp.broadcast_to(jnp.sum(jnp.where(line == lane, values, 0), axis=1, keepdims=True), (rec_dev, LANES))

    across[...] = jnp.zeros_like(across)
    own_t = widened(owner, 0)
    own = upright(own_t)
    first, last = upright(widened(valid, 0)), upright(widened(valid, 1))
    bins[...] = jnp.zeros_like(bins)
    bins[:, pl.ds(0, BINS)] = mask[...].astype(f32)
    before = listed & (lane < line)

    def count(what):
        return jnp.broadcast_to(jnp.sum(jnp.where(what, 1, 0), axis=1, keepdims=True), (rec_dev, LANES))

    def count_t(what):
        return jnp.broadcast_to(jnp.sum(jnp.where(what, 1, 0), axis=0, keepdims=True), (rec_dev, LANES))

    far = lax.rem(own // 2 + chips - z, chips)
    far_t = lax.rem(own_t // 2 + chips - z, chips)
    rank = count(before & (own_t == own))
    turn = count(before & (far_t == half))
    turn_t = count_t((line < lane) & (far == half))
    up = ((far > 0) & (far < half)) | ((far == half) & (turn % 2 == 0))
    up_t = ((far_t > 0) & (far_t < half)) | ((far_t == half) & (turn_t % 2 == 0))
    down = (far > half) | ((far == half) & (turn % 2 == 1))
    down_t = (far_t > half) | ((far_t == half) & (turn_t % 2 == 1))
    same = before & (far_t == far)
    place_up = count(listed & up_t & ((far_t > far) | same))
    place_down = count(listed & down_t & ((far_t < far) | same))
    place = jnp.where(up, place_up, jnp.where(down, rec_dev + place_down, line))
    key = far * (2 * MOST) + (own % 2) * MOST + rank
    sent = jnp.sum(jnp.where(key == lane, place + 1, 0), axis=0, keepdims=True)
    meta_out[...] = jnp.broadcast_to(sent, meta_out.shape)
    taken = jnp.sum(jnp.where((place == lane) & (up | down), line, 0), axis=0, keepdims=True)
    order[...] = jnp.broadcast_to(taken, order.shape)
    order_copy = pltpu.make_async_copy(order, order_s, local.at[0])
    order_copy.start()
    own_copy = pltpu.make_async_copy(meta_out, meta_s.at[0], local.at[1])
    own_copy.start()

    rec_copy.wait()
    for s in (1, 0):
        for b in range(frames):
            for c in range(comps):
                ext[s, MARGIN + b, pl.ds(c * rec_dev, rec_dev), :] = rec[s, c, :, pl.ds(b * HOP, HOP)]

    pl.semaphore_wait(barrier, len(others))

    halo = []
    for i, s in enumerate((1, 0)):
        halo.append(send(ext.at[s, pl.ds(frames, MARGIN)], ext.at[s, pl.ds(0, MARGIN)],
                         halo_send.at[2 * i], halo_recv.at[2 * i], band(1)))
        halo.append(send(ext.at[s, pl.ds(MARGIN, MARGIN)], ext.at[s, pl.ds(MARGIN + frames, MARGIN)],
                         halo_send.at[2 * i + 1], halo_recv.at[2 * i + 1], band(-1)))
    for d in range(1, chips):
        send(meta_out, meta_in.at[d - 1], one_send.at[0], one_recv.at[0], chip(d))

    def analyse(s):
        total = None
        for tap in range(TAPS):
            term = jnp.dot(
                ext[s, pl.ds(tap, frames)].reshape(frames * traces, HOP),
                table[pl.ds(tap * HOP, HOP), :],
                preferred_element_type=f32,
            )
            total = term if total is None else total + term
        coef[s] = total.astype(jnp.bfloat16)

    def take_halo(i, s):
        halo[2 * i].wait_recv()
        halo[2 * i + 1].wait_recv()

        @pl.when(t == 0)
        def _():
            ext[s, pl.ds(0, MARGIN)] = jnp.zeros((MARGIN, traces, HOP), jnp.bfloat16)

        @pl.when(t == groups - 1)
        def _():
            ext[s, pl.ds(MARGIN + frames, MARGIN)] = jnp.zeros((MARGIN, traces, HOP), jnp.bfloat16)

    table_copy.wait()
    take_halo(0, 1)
    analyse(1)
    diagonal = lax.broadcasted_iota(i32, (traces, LANES), 0) == lax.broadcasted_iota(i32, (traces, LANES), 1)
    power = jnp.zeros((traces, LANES), f32)
    for f in range(frames):
        o = coef[1, pl.ds(f * traces, traces), :].astype(f32)
        power = power + (o[:, :LANES] * o[:, :LANES] + o[:, LANES:] * o[:, LANES:])
    power = jnp.broadcast_to(jnp.sum(power, axis=1, keepdims=True), (traces, LANES))
    power = jnp.sum(jnp.where(diagonal, power, 0.0), axis=0, keepdims=True)
    lv_out[...] = jnp.broadcast_to(power, lv_out.shape)
    for d in range(1, groups):
        send(lv_out, lv_in.at[d - 1], one_send.at[1], one_recv.at[1], band(d))

    take_halo(1, 0)
    analyse(0)

    wait_bytes(lv_in, one_recv.at[1])
    power = lv_out[...]
    for d in range(1, groups):
        power = power + lv_in[d - 1]
    power = jnp.broadcast_to(power[0:1], (traces, LANES))
    power = jnp.sum(jnp.where(diagonal, power, 0.0), axis=1, keepdims=True)
    level = jnp.broadcast_to(WATER * (power / (frames * groups * BINS)) + EPSILON, (traces, LANES))

    first, last, bands = (jnp.concatenate([v] * comps, axis=0) for v in (first, last, bins[...]))
    for f in range(frames):
        center = (t * frames + f) * HOP + HOP // 2
        weight = jnp.where((first <= center) & (center < last), bands, 0.0)
        x = coef[0, pl.ds(f * traces, traces), :].astype(f32)
        y = coef[1, pl.ds(f * traces, traces), :].astype(f32)
        x_re, x_im, y_re, y_im = x[:, :LANES], x[:, LANES:], y[:, :LANES], y[:, LANES:]
        x_inv = lax.rsqrt(x_re * x_re + x_im * x_im + level)
        y_inv = lax.rsqrt(y_re * y_re + y_im * y_im + level)
        d_re = weight * (x_re * x_inv - y_re * y_inv)
        d_im = weight * (x_im * x_inv - y_im * y_inv)
        inner = (x_re * d_re + x_im * d_im) * (x_inv * x_inv * x_inv)
        adj[pl.ds(f * traces, traces), pl.ds(0, LANES)] = (d_re * x_inv - x_re * inner).astype(jnp.bfloat16)
        adj[pl.ds(f * traces, traces), pl.ds(LANES, LANES)] = (d_im * x_inv - x_im * inner).astype(jnp.bfloat16)

    acc[...] = jnp.zeros_like(acc)
    for tap in range(TAPS):
        term = lax.dot_general(
            adj[...], table[pl.ds(tap * HOP, HOP), :], (((1,), (1,)), ((), ())), preferred_element_type=f32
        )
        acc[pl.ds(tap, frames)] += term.reshape(frames, traces, HOP)
    edge_out[0] = acc[pl.ds(MARGIN + frames, MARGIN)].astype(jnp.bfloat16)
    edge_out[1] = acc[pl.ds(0, MARGIN)].astype(jnp.bfloat16)
    edges = [
        send(edge_out.at[i], edge_in.at[i], edge_send.at[i], edge_recv.at[i], band(1 - 2 * i)) for i in range(2)
    ]
    for edge in edges:
        edge.wait_recv()
    for b in range(frames):
        side, i = (0, b) if b < MARGIN else (1, b - MARGIN)
        inner_band = (t > 0) if side == 0 else (t < groups - 1)
        more = jnp.where(inner_band, edge_in[side, i].astype(f32), 0.0)
        block = acc[MARGIN + b] + more
        for h in range(HOP // LANES):
            j = b * (HOP // LANES) + h
            flat[pl.ds(j * traces, traces), :] = block[:, h * LANES : (h + 1) * LANES]

    order_copy.wait()
    own_copy.wait()
    for c in range(comps):
        for r in range(rec_dev):
            row = flat[pl.ds(c * rec_dev + r, per_row, stride=traces), :]
            rows[c, r] = row.astype(jnp.bfloat16)
    flying = {}

    def hop(k, c, i):
        src = packet.at[i, c] if k == 1 else bufs[2 * (k - 2) + i].at[c, pl.ds(0, hops[k - 1])]
        n = ((k - 1) * comps + c) * 2 + i
        flying[k, c, i] = send(src, bufs[2 * (k - 1) + i].at[c], ring_send.at[n], ring_recv.at[n], chip(1 - 2 * i))

    for c in range(comps):
        for i in range(2):
            for p in range(rec_dev):
                packet[i, c, p] = rows[c, order_s[0, i * rec_dev + p]]
            hop(1, c, i)

    wait_bytes(meta_in, one_recv.at[0])
    got = pltpu.make_async_copy(meta_in, meta_s.at[pl.ds(1, chips - 1)], local.at[2])
    got.start()
    got.wait()

    def keep(source, rank, c, row):
        slot = (lax.rem(z + source + chips, chips) * 2 + core) * MOST + rank
        slots[pl.ds(pl.multiple_of((slot * comps + c) * per_row, per_row), per_row), :] = row.astype(f32)

    def deal(source, j, read):
        for e in range(2 * MOST):
            mine, rank = e // MOST == 0, e % MOST
            whose = core if mine else 1 - core
            away = (-source) % chips
            v = meta_s[away, 0, away * 2 * MOST + whose * MOST + rank]
            for c in range(comps):
                row = jnp.where(v > 0, read(c, v), jnp.zeros((), jnp.bfloat16))
                if mine:
                    keep(source, rank, c, row)
                else:
                    mate_out[j, rank, c] = row

    def from_ring(k, i):
        def read(c, v):
            at = jnp.clip(v - 1 - i * rec_dev, 0, hops[k - 1] - 1)
            return bufs[2 * (k - 1) + i][c, at]

        return read

    def from_both(c, v):
        return jnp.where(v > rec_dev, from_ring(half, 1)(c, v), from_ring(half, 0)(c, v))

    deal(0, 0, lambda c, v: rows[c, jnp.clip(v - 1, 0, rec_dev - 1)])
    mates = []

    def to_mate(first_j, number):
        ref = (mate_out.at[pl.ds(first_j, number)], mate_in.at[pl.ds(first_j, number)])
        mates.append((first_j, number, send(*ref, one_send.at[2], mate_recv.at[len(mates)], mate)))

    for k in range(2, half + 2):
        for c in range(comps):
            for i in range(2):
                flying[k - 1, c, i].wait_recv()
                if k <= half:
                    hop(k, c, i)
        if k <= half:
            for i in range(2):
                deal(1 - k if i == 0 else k - 1, 2 * (k - 1) - 1 + i, from_ring(k - 1, i))
            if k % 2 == 0:
                to_mate(2 * (k - 2) - 1 if k > 2 else 0, 4 if k > 2 else 3)
        else:
            deal(half, 2 * half - 1, from_both)
            to_mate(2 * half - 1, 1)
    source_of = [0] + [s for k in range(1, half) for s in (-k, k)] + [half]
    for first_j, number, copy in mates:
        copy.wait_recv()
        for j in range(first_j, first_j + number):
            for rank in range(MOST):
                slot = (lax.rem(z + source_of[j] + chips, chips) * 2 + 1 - core) * MOST + rank
                for c in range(comps):
                    slots[pl.ds(pl.multiple_of((slot * comps + c) * per_row, per_row), per_row), :] = (
                        mate_in[j, rank, c].astype(f32)
                    )
    kept = chips * 2 * MOST
    for c in range(comps):
        for j in range(per_row):
            part = slots[pl.ds(c * per_row + j, kept, stride=comps * per_row), :]
            out[c, :, pl.ds(j * LANES, LANES)] = part.astype(jnp.bfloat16)

    for copy in halo + edges + list(flying.values()):
        copy.wait_send()
    wait_bytes(meta_in, one_send.at[0])
    wait_bytes(lv_in, one_send.at[1])
    wait_bytes(mate_out, one_send.at[2])


def solution(mesh):
    chips, groups = mesh.shape["space"] // 2, mesh.shape["tm"]

    def on_device(recordings, owner, valid_range, bin_mask):
        _, comps, rec_dev, samples = recordings.shape
        frames = samples // HOP
        traces, per_row = comps * rec_dev, samples // LANES
        kept = chips * 2 * MOST
        bf16, f32, i32 = jnp.bfloat16, jnp.float32, jnp.int32
        sizes = (chips, groups, comps, rec_dev, frames)
        dma = pltpu.SemaphoreType.DMA
        return pl.pallas_call(
            functools.partial(kernel, sizes),
            out_shape=jax.ShapeDtypeStruct((comps, kept, samples), bf16),
            in_specs=[pl.BlockSpec(memory_space=space) for space in (pl.ANY, pltpu.VMEM, pltpu.VMEM, pltpu.VMEM, pl.ANY)],
            out_specs=pl.BlockSpec(memory_space=pltpu.VMEM),
            scratch_shapes=[
                pltpu.VMEM(recordings.shape, bf16),
                pltpu.VMEM((KERNEL, 2 * LANES), bf16),
                pltpu.VMEM((rec_dev, LANES), f32),
                pltpu.VMEM((8, LANES), i32),
                pltpu.VMEM((2, frames + 2 * MARGIN, traces, HOP), bf16),
                pltpu.VMEM((2, frames * traces, 2 * LANES), bf16),
                pltpu.VMEM((frames * traces, 2 * LANES), bf16),
                pltpu.VMEM((frames + 2 * MARGIN, traces, HOP), f32),
                pltpu.VMEM((8, LANES), f32),
                pltpu.VMEM((groups - 1, 8, LANES), f32),
                pltpu.VMEM((8, LANES), i32),
                pltpu.VMEM((chips - 1, 8, LANES), i32),
                pltpu.VMEM((8, LANES), i32),
                pltpu.SMEM((chips, 8, LANES), i32),
                pltpu.SMEM((8, LANES), i32),
                pltpu.VMEM((2, MARGIN, traces, HOP), bf16),
                pltpu.VMEM((2, MARGIN, traces, HOP), bf16),
                pltpu.VMEM((per_row * traces, LANES), f32),
                pltpu.VMEM((comps, rec_dev, per_row, LANES), bf16),
                pltpu.VMEM((2, comps, rec_dev, per_row, LANES), bf16),
                pltpu.VMEM((chips, MOST, comps, per_row, LANES), bf16),
                pltpu.VMEM((chips, MOST, comps, per_row, LANES), bf16),
                pltpu.VMEM((kept * comps * per_row, LANES), f32),
                dma((4,)), dma((4,)), dma((3,)), dma((2,)), dma((2,)), dma((2,)),
                dma((chips * comps,)), dma((chips * comps,)), dma((chips // 4 + 1,)), dma((5,)),
            ] + [pltpu.VMEM((comps, n, per_row, LANES), bf16) for n in ring_rows(chips, rec_dev) for _ in range(2)],
            compiler_params=pltpu.CompilerParams(
                collective_id=0, has_side_effects=True, vmem_limit_bytes=60 << 20
            ),
        )(recordings, owner.T, valid_range.T, bin_mask, jnp.asarray(cq_table()))

    return jax.shard_map(
        on_device,
        mesh=mesh,
        in_specs=(
            P(None, None, "space", "tm"),
            P("space", None),
            P("space", None),
            P("space", None),
        ),
        out_specs=P(None, "space", "tm"),
        check_vma=False,
    )
```

```python
import functools
import math

import jax
import jax.numpy as jnp
import ml_dtypes
import numpy as np
from jax import lax
from jax.experimental import pallas as pl
from jax.experimental.pallas import tpu as pltpu
from jax.sharding import PartitionSpec as P

BINS = 96
HOP = 256
HALO = 1024
KERNEL = 2304
TAPS = KERNEL // HOP
MARGIN = HALO // HOP
WATER = 0.1
EPSILON = 1e-06
MOST = 2
LANES = 128
MESH = pl.DeviceIdType.MESH


def cq_table():
    f32 = np.float32
    octave_bins = BINS // 8
    index = np.arange(BINS).astype(f32)
    freq = f32(0.25) * np.exp2(((index - f32(BINS - 1)) / f32(octave_bins)).astype(np.float64)).astype(f32)
    quality = f32(1.0 / (2.0 ** (1.0 / octave_bins) - 1.0))
    support = np.minimum(quality / freq, f32(KERNEL))
    offset = np.arange(KERNEL).astype(f32) - f32(0.5 * (KERNEL - 1))
    ratio = (offset[:, None] / support[None, :]).astype(np.float64)
    window = np.where(np.abs(ratio) < 0.5, 0.5 + 0.5 * np.cos(2.0 * math.pi * ratio), 0.0)
    window = window / np.sqrt(np.sum(window * window, axis=0, keepdims=True))
    cycles = offset[:, None] * freq[None, :]
    phase = (cycles - np.floor(cycles)).astype(np.float64)
    table = np.zeros((KERNEL, 2 * LANES))
    table[:, :BINS] = window * np.cos(2.0 * math.pi * phase)
    table[:, LANES : LANES + BINS] = -window * np.sin(2.0 * math.pi * phase)
    return table.astype(f32).astype(ml_dtypes.bfloat16)


def ring_rows(chips, rec_dev):
    half = chips // 2
    return [min(rec_dev, 2 * MOST * (half - k) + MOST) for k in range(1, half + 1)]


def ring_groups(hops):
    depth = [sum(n > p for n in hops) for p in range(hops[0])]
    firsts = [p for p in range(len(depth)) if p == 0 or depth[p] != depth[p - 1]] + [len(depth)]
    return [(a, b - a, depth[a]) for a, b in zip(firsts[:-1], firsts[1:])]


def kernel(
    sizes, rec_in, owner, valid, mask, table_in, out, table, bins, across,
    ext, coef, adj, acc, lv_out, lv_in, meta_out, meta_in, order, meta_s, order_s,
    flat, rows, packet, mate_out, mate_in, slots,
    halo_send, halo_recv, one_send, one_recv, ring_send, ring_recv, mate_recv, local, *bufs,
):
    chips, groups, comps, rec_dev, frames = sizes
    half = chips // 2
    traces = comps * rec_dev
    per_row = frames * HOP // LANES
    hops = ring_rows(chips, rec_dev)
    parts = ring_groups(hops)
    samples = frames * HOP
    f32, i32 = jnp.float32, jnp.int32

    space, t = lax.axis_index("space"), lax.axis_index("tm")
    z, core = space // 2, space % 2

    def band(d):
        return {"tm": lax.rem(t + d + groups, groups)}

    def chip(d):
        return {"space": lax.rem(z + d + chips, chips) * 2 + core}

    mate = {"space": z * 2 + 1 - core}

    def send(src, dst, ss, rs, to):
        copy = pltpu.make_async_remote_copy(src, dst, ss, rs, device_id=to, device_id_type=MESH)
        copy.start()
        return copy

    def wait_bytes(ref, sem):
        pltpu.make_async_copy(ref, ref, sem).wait()

    barrier = pltpu.get_barrier_semaphore()
    others = [band(d) for d in range(1, groups)] + [chip(d) for d in range(1, chips)] + [mate]
    for to in others:
        pl.semaphore_signal(barrier, inc=1, device_id=to, device_id_type=MESH)

    rec_copy = pltpu.make_async_copy(rec_in, ext.at[:, :, :, pl.ds(2 * HALO, samples)], local.at[3])
    rec_copy.start()
    table_copy = pltpu.make_async_copy(table_in, table, local.at[4])
    table_copy.start()

    pl.semaphore_wait(barrier, len(others))

    halo = {}
    after = 2 * HALO + samples
    for part, s in ((0, 1), (0, 0), (1, 1), (1, 0)):
        for side in range(2):
            at, to = [
                [(samples - HALO, HALO), (samples - 2 * HALO, 0)],
                [(0, after), (HALO, after + HALO)],
            ][side][part]
            n = (part * 2 + s) * 2 + side
            halo[part, s, side] = send(
                rec_in.at[s, :, :, pl.ds(at, HALO)], ext.at[s, :, :, pl.ds(to, HALO)],
                halo_send.at[n], halo_recv.at[n], band(1 - 2 * side),
            )

    def analyse(s, first_f, number):
        blocks = [
            jnp.concatenate([ext[s, c, :, pl.ds((first_f + b) * HOP, HOP)] for c in range(comps)], axis=0)
            for b in range(number + 2 * MARGIN)
        ]
        total = None
        for tap in range(TAPS):
            term = jnp.dot(
                jnp.concatenate(blocks[tap : tap + number], axis=0),
                table[pl.ds(tap * HOP, HOP), :],
                preferred_element_type=f32,
            )
            total = term if total is None else total + term
        coef[s, pl.ds(first_f * traces, number * traces), :] = total.astype(jnp.bfloat16)

    def take_halo(part, s):
        halo[part, s, 0].wait_recv()
        halo[part, s, 1].wait_recv()
        low = (1 - part) * HALO

        @pl.when(t == 0)
        def _():
            ext[s, :, :, pl.ds(low, HALO)] = jnp.zeros((comps, rec_dev, HALO), jnp.bfloat16)

        @pl.when(t == groups - 1)
        def _():
            ext[s, :, :, pl.ds(after + part * HALO, HALO)] = jnp.zeros((comps, rec_dev, HALO), jnp.bfloat16)

    table_copy.wait()
    rec_copy.wait()
    take_halo(0, 1)
    analyse(1, MARGIN, frames)
    diagonal = lax.broadcasted_iota(i32, (traces, LANES), 0) == lax.broadcasted_iota(i32, (traces, LANES), 1)
    power = jnp.zeros((traces, LANES), f32)
    for f in range(frames):
        o = coef[1, pl.ds((MARGIN + f) * traces, traces), :].astype(f32)
        power = power + (o[:, :LANES] * o[:, :LANES] + o[:, LANES:] * o[:, LANES:])
    power = jnp.broadcast_to(jnp.sum(power, axis=1, keepdims=True), (traces, LANES))
    power = jnp.sum(jnp.where(diagonal, power, 0.0), axis=0, keepdims=True)
    lv_out[...] = jnp.broadcast_to(power, lv_out.shape)
    for d in range(1, groups):
        send(lv_out, lv_in.at[d - 1], one_send.at[1], one_recv.at[1], band(d))
    lane = lax.broadcasted_iota(i32, (rec_dev, LANES), 1)
    line = lax.broadcasted_iota(i32, (rec_dev, LANES), 0)
    listed = lane < rec_dev

    def widened(ref, n):
        across[n : n + 1, pl.ds(0, rec_dev)] = ref[n : n + 1, :]
        return jnp.broadcast_to(across[n : n + 1, :], (rec_dev, LANES))

    def upright(values):
        return jnp.broadcast_to(jnp.sum(jnp.where(line == lane, values, 0), axis=1, keepdims=True), (rec_dev, LANES))

    across[...] = jnp.zeros_like(across)
    own_t = widened(owner, 0)
    own = upright(own_t)
    first, last = upright(widened(valid, 0)), upright(widened(valid, 1))
    bins[...] = jnp.zeros_like(bins)
    bins[:, pl.ds(0, BINS)] = mask[...].astype(f32)
    before = listed & (lane < line)

    def count(what):
        return jnp.broadcast_to(jnp.sum(jnp.where(what, 1, 0), axis=1, keepdims=True), (rec_dev, LANES))

    def count_t(what):
        return jnp.broadcast_to(jnp.sum(jnp.where(what, 1, 0), axis=0, keepdims=True), (rec_dev, LANES))

    far = lax.rem(own // 2 + chips - z, chips)
    far_t = lax.rem(own_t // 2 + chips - z, chips)
    rank = count(before & (own_t == own))
    turn = count(before & (far_t == half))
    turn_t = count_t((line < lane) & (far == half))
    up = ((far > 0) & (far < half)) | ((far == half) & (turn % 2 == 0))
    up_t = ((far_t > 0) & (far_t < half)) | ((far_t == half) & (turn_t % 2 == 0))
    down = (far > half) | ((far == half) & (turn % 2 == 1))
    down_t = (far_t > half) | ((far_t == half) & (turn_t % 2 == 1))
    same = before & (far_t == far)
    place_up = count(listed & up_t & ((far_t > far) | same))
    place_down = count(listed & down_t & ((far_t < far) | same))
    place = jnp.where(up, place_up, jnp.where(down, rec_dev + place_down, line))
    key = far * (2 * MOST) + (own % 2) * MOST + rank
    sent = jnp.sum(jnp.where(key == lane, place + 1, 0), axis=0, keepdims=True)
    meta_out[...] = jnp.broadcast_to(sent, meta_out.shape)
    taken = jnp.sum(jnp.where((place == lane) & (up | down), line, 0), axis=0, keepdims=True)
    order[...] = jnp.broadcast_to(taken, order.shape)
    order_copy = pltpu.make_async_copy(order, order_s, local.at[0])
    order_copy.start()
    own_copy = pltpu.make_async_copy(meta_out, meta_s.at[0], local.at[1])
    own_copy.start()
    for d in range(1, chips):
        send(meta_out, meta_in.at[d - 1], one_send.at[0], one_recv.at[0], chip(d))

    take_halo(0, 0)
    analyse(0, MARGIN, frames)
    for s in (1, 0):
        take_halo(1, s)
        analyse(s, 0, MARGIN)
        analyse(s, MARGIN + frames, MARGIN)

    wait_bytes(lv_in, one_recv.at[1])
    power = lv_out[...]
    for d in range(1, groups):
        power = power + lv_in[d - 1]
    power = jnp.broadcast_to(power[0:1], (traces, LANES))
    power = jnp.sum(jnp.where(diagonal, power, 0.0), axis=1, keepdims=True)
    level = jnp.broadcast_to(WATER * (power / (frames * groups * BINS)) + EPSILON, (traces, LANES))

    first, last, bands = (jnp.concatenate([v] * comps, axis=0) for v in (first, last, bins[...]))
    for f in range(frames + 2 * MARGIN):
        center = (t * frames + f - MARGIN) * HOP + HOP // 2
        weight = jnp.where((first <= center) & (center < last), bands, 0.0)
        x = coef[0, pl.ds(f * traces, traces), :].astype(f32)
        y = coef[1, pl.ds(f * traces, traces), :].astype(f32)
        x_re, x_im, y_re, y_im = x[:, :LANES], x[:, LANES:], y[:, :LANES], y[:, LANES:]
        x_inv = lax.rsqrt(x_re * x_re + x_im * x_im + level)
        y_inv = lax.rsqrt(y_re * y_re + y_im * y_im + level)
        d_re = weight * (x_re * x_inv - y_re * y_inv)
        d_im = weight * (x_im * x_inv - y_im * y_inv)
        inner = (x_re * d_re + x_im * d_im) * (x_inv * x_inv * x_inv)
        adj[pl.ds(f * traces, traces), pl.ds(0, LANES)] = (d_re * x_inv - x_re * inner).astype(jnp.bfloat16)
        adj[pl.ds(f * traces, traces), pl.ds(LANES, LANES)] = (d_im * x_inv - x_im * inner).astype(jnp.bfloat16)

    for tap in range(TAPS):
        term = lax.dot_general(
            adj[pl.ds((2 * MARGIN - tap) * traces, frames * traces), :], table[pl.ds(tap * HOP, HOP), :],
            (((1,), (1,)), ((), ())), preferred_element_type=f32,
        )
        acc[...] = term if tap == 0 else acc[...] + term
    for b in range(frames):
        block = acc[pl.ds(b * traces, traces), :]
        for h in range(HOP // LANES):
            j = b * (HOP // LANES) + h
            flat[pl.ds(j * traces, traces), :] = block[:, h * LANES : (h + 1) * LANES]

    order_copy.wait()
    own_copy.wait()
    for c in range(comps):
        for r in range(rec_dev):
            row = flat[pl.ds(c * rec_dev + r, per_row, stride=traces), :]
            rows[r, pl.ds(c * per_row, per_row), :] = row.astype(jnp.bfloat16)
    flying = {}

    def hop(k, g, i):
        first_p, number, _ = parts[g]
        run = pl.ds(first_p, number)
        src = packet.at[i, run] if k == 1 else bufs[2 * (k - 2) + i].at[run]
        if k > 2:
            flying[k - 2, g, i].wait_send()
        flying[k, g, i] = send(
            src, bufs[2 * (k - 1) + i].at[run], ring_send.at[(g * 2 + k % 2) * 2 + i],
            ring_recv.at[((k - 1) * len(parts) + g) * 2 + i], chip(1 - 2 * i),
        )

    for g, (first_p, number, _) in enumerate(parts):
        for i in range(2):
            for p in range(first_p, first_p + number):
                packet[i, p] = rows[order_s[0, i * rec_dev + p]]
            hop(1, g, i)

    wait_bytes(meta_in, one_recv.at[0])
    got = pltpu.make_async_copy(meta_in, meta_s.at[pl.ds(1, chips - 1)], local.at[2])
    got.start()
    got.wait()

    whole = comps * per_row

    def keep(source, rank, row, whose):
        slot = (lax.rem(z + source + chips, chips) * 2 + whose) * MOST + rank
        slots[pl.ds(pl.multiple_of(slot * whole, whole), whole), :] = row.astype(f32)

    def deal(source, j, read):
        for e in range(2 * MOST):
            mine, rank = e // MOST == 0, e % MOST
            whose = core if mine else 1 - core
            away = (-source) % chips
            v = meta_s[away, 0, away * 2 * MOST + whose * MOST + rank]
            row = jnp.where(v > 0, read(v), jnp.zeros((), jnp.bfloat16))
            if mine:
                keep(source, rank, row, core)
            else:
                mate_out[j, rank] = row

    def from_ring(k, i):
        def read(v):
            at = jnp.clip(v - 1 - i * rec_dev, 0, hops[k - 1] - 1)
            return bufs[2 * (k - 1) + i][at]

        return read

    def from_both(v):
        return jnp.where(v > rec_dev, from_ring(half, 1)(v), from_ring(half, 0)(v))

    deal(0, 0, lambda v: rows[jnp.clip(v - 1, 0, rec_dev - 1)])
    mates = []

    def to_mate(first_j, number):
        ref = (mate_out.at[pl.ds(first_j, number)], mate_in.at[pl.ds(first_j, number)])
        mates.append((first_j, number, send(*ref, one_send.at[2], mate_recv.at[len(mates)], mate)))

    steps = sorted((k / (depth + 2), g, k) for g, (_, _, depth) in enumerate(parts) for k in range(1, depth + 1))
    waits = {k: sum(depth >= k for _, _, depth in parts) for k in range(1, half + 1)}
    ready = 1
    for _, g, k in steps:
        for i in range(2):
            flying[k, g, i].wait_recv()
            if k < parts[g][2]:
                hop(k + 1, g, i)
        waits[k] -= 1
        while ready < half and waits[ready] == 0:
            for i in range(2):
                deal(-ready if i == 0 else ready, 2 * ready - 1 + i, from_ring(ready, i))
            if ready % 2 == 1 and ready > 1:
                to_mate(*((0, 7) if ready == 3 else (2 * ready - 3, 4)))
            ready += 1
    deal(half, 2 * half - 1, from_both)
    to_mate(2 * half - 1, 1)
    source_of = [0] + [s for k in range(1, half) for s in (-k, k)] + [half]
    for first_j, number, copy in mates:
        copy.wait_recv()
        for j in range(first_j, first_j + number):
            for rank in range(MOST):
                keep(source_of[j], rank, mate_in[j, rank], 1 - core)
    kept = chips * 2 * MOST
    for c in range(comps):
        for j in range(per_row):
            part = slots[pl.ds(c * per_row + j, kept, stride=whole), :]
            out[c, :, pl.ds(j * LANES, LANES)] = part.astype(jnp.bfloat16)

    for copy in halo.values():
        copy.wait_send()
    for g, (_, _, depth) in enumerate(parts):
        for k in range(max(1, depth - 1), depth + 1):
            for i in range(2):
                flying[k, g, i].wait_send()
    wait_bytes(meta_in, one_send.at[0])
    wait_bytes(lv_in, one_send.at[1])
    wait_bytes(mate_out, one_send.at[2])


def solution(mesh):
    chips, groups = mesh.shape["space"] // 2, mesh.shape["tm"]

    def on_device(recordings, owner, valid_range, bin_mask):
        _, comps, rec_dev, samples = recordings.shape
        frames = samples // HOP
        traces, per_row = comps * rec_dev, samples // LANES
        kept = chips * 2 * MOST
        hops = ring_rows(chips, rec_dev)
        parts = len(ring_groups(hops))
        bf16, f32, i32 = jnp.bfloat16, jnp.float32, jnp.int32
        sizes = (chips, groups, comps, rec_dev, frames)
        dma = pltpu.SemaphoreType.DMA
        return pl.pallas_call(
            functools.partial(kernel, sizes),
            out_shape=jax.ShapeDtypeStruct((comps, kept, samples), bf16),
            in_specs=[pl.BlockSpec(memory_space=space) for space in (pl.ANY, pltpu.VMEM, pltpu.VMEM, pltpu.VMEM, pl.ANY)],
            out_specs=pl.BlockSpec(memory_space=pltpu.VMEM),
            scratch_shapes=[
                pltpu.VMEM((KERNEL, 2 * LANES), bf16),
                pltpu.VMEM((rec_dev, LANES), f32),
                pltpu.VMEM((8, LANES), i32),
                pltpu.VMEM((2, comps, rec_dev, samples + 4 * HALO), bf16),
                pltpu.VMEM((2, (frames + 2 * MARGIN) * traces, 2 * LANES), bf16),
                pltpu.VMEM(((frames + 2 * MARGIN) * traces, 2 * LANES), bf16),
                pltpu.VMEM((frames * traces, HOP), f32),
                pltpu.VMEM((8, LANES), f32),
                pltpu.VMEM((groups - 1, 8, LANES), f32),
                pltpu.VMEM((8, LANES), i32),
                pltpu.VMEM((chips - 1, 8, LANES), i32),
                pltpu.VMEM((8, LANES), i32),
                pltpu.SMEM((chips, 8, LANES), i32),
                pltpu.SMEM((8, LANES), i32),
                pltpu.VMEM((per_row * traces, LANES), f32),
                pltpu.VMEM((rec_dev, comps * per_row, LANES), bf16),
                pltpu.VMEM((2, rec_dev, comps * per_row, LANES), bf16),
                pltpu.VMEM((chips, MOST, comps * per_row, LANES), bf16),
                pltpu.VMEM((chips, MOST, comps * per_row, LANES), bf16),
                pltpu.VMEM((kept * comps * per_row, LANES), f32),
                dma((8,)), dma((8,)), dma((3,)), dma((2,)),
                dma((4 * parts,)), dma((chips * parts,)), dma((chips // 4,)), dma((5,)),
            ] + [pltpu.VMEM((n, comps * per_row, LANES), bf16) for n in hops for _ in range(2)],
            compiler_params=pltpu.CompilerParams(
                collective_id=0, has_side_effects=True, vmem_limit_bytes=60 << 20
            ),
        )(recordings, owner.T, valid_range.T, bin_mask, jnp.asarray(cq_table()))

    return jax.shard_map(
        on_device,
        mesh=mesh,
        in_specs=(
            P(None, None, "space", "tm"),
            P("space", None),
            P("space", None),
            P("space", None),
        ),
        out_specs=P(None, "space", "tm"),
        check_vma=False,
    )
```

```python
import functools
import math

import jax
import jax.numpy as jnp
import ml_dtypes
import numpy as np
from jax import lax
from jax.experimental import pallas as pl
from jax.experimental.pallas import tpu as pltpu
from jax.sharding import PartitionSpec as P

BINS = 96
HOP = 256
HALO = 1024
KERNEL = 2304
TAPS = KERNEL // HOP
MARGIN = HALO // HOP
WATER = 0.1
EPSILON = 1e-06
MOST = 2
LANES = 128
MESH = pl.DeviceIdType.MESH


def cq_table():
    f32 = np.float32
    octave_bins = BINS // 8
    index = np.arange(BINS).astype(f32)
    freq = f32(0.25) * np.exp2(((index - f32(BINS - 1)) / f32(octave_bins)).astype(np.float64)).astype(f32)
    quality = f32(1.0 / (2.0 ** (1.0 / octave_bins) - 1.0))
    support = np.minimum(quality / freq, f32(KERNEL))
    offset = np.arange(KERNEL).astype(f32) - f32(0.5 * (KERNEL - 1))
    ratio = (offset[:, None] / support[None, :]).astype(np.float64)
    window = np.where(np.abs(ratio) < 0.5, 0.5 + 0.5 * np.cos(2.0 * math.pi * ratio), 0.0)
    window = window / np.sqrt(np.sum(window * window, axis=0, keepdims=True))
    cycles = offset[:, None] * freq[None, :]
    phase = (cycles - np.floor(cycles)).astype(np.float64)
    table = np.zeros((KERNEL, 2 * LANES))
    table[:, :BINS] = window * np.cos(2.0 * math.pi * phase)
    table[:, LANES : LANES + BINS] = -window * np.sin(2.0 * math.pi * phase)
    return table.astype(f32).astype(ml_dtypes.bfloat16)


def ring_rows(chips, rec_dev):
    half = chips // 2
    return [min(rec_dev, 2 * MOST * (half - k) + MOST) for k in range(1, half + 1)]


def ring_groups(hops):
    depth = [sum(n > p for n in hops) for p in range(hops[0])]
    firsts = [p for p in range(len(depth)) if p == 0 or depth[p] != depth[p - 1]] + [len(depth)]
    return [(a, b - a, depth[a]) for a, b in zip(firsts[:-1], firsts[1:])]


def kernel(
    sizes, rec_in, owner, valid, mask, table_in, out, table, bins, across,
    ext, coef, adj, acc, lv_out, lv_in, meta_out, meta_in, order, meta_s, order_s,
    flat, rows, packet, mate_out, mate_in, slots,
    halo_send, halo_recv, one_send, one_recv, ring_send, ring_recv, mate_recv, local, *bufs,
):
    chips, groups, comps, rec_dev, frames = sizes
    half = chips // 2
    traces = comps * rec_dev
    per_row = frames * HOP // LANES
    hops = ring_rows(chips, rec_dev)
    parts = ring_groups(hops)
    samples = frames * HOP
    f32, i32 = jnp.float32, jnp.int32

    space, t = lax.axis_index("space"), lax.axis_index("tm")
    z, core = space // 2, space % 2

    def band(d):
        return {"tm": lax.rem(t + d + groups, groups)}

    def chip(d):
        return {"space": lax.rem(z + d + chips, chips) * 2 + core}

    mate = {"space": z * 2 + 1 - core}

    def send(src, dst, ss, rs, to):
        copy = pltpu.make_async_remote_copy(src, dst, ss, rs, device_id=to, device_id_type=MESH)
        copy.start()
        return copy

    def wait_bytes(ref, sem):
        pltpu.make_async_copy(ref, ref, sem).wait()

    barrier = pltpu.get_barrier_semaphore()
    others = [band(d) for d in range(1, groups)] + [chip(d) for d in range(1, chips)] + [mate]
    for to in others:
        pl.semaphore_signal(barrier, inc=1, device_id=to, device_id_type=MESH)

    rec_copy = pltpu.make_async_copy(rec_in, ext.at[:, :, :, pl.ds(2 * HALO, samples)], local.at[3])
    rec_copy.start()
    table_copy = pltpu.make_async_copy(table_in, table, local.at[4])
    table_copy.start()

    pl.semaphore_wait(barrier, len(others))

    halo = {}
    after = 2 * HALO + samples
    for part, s in ((0, 1), (0, 0), (1, 1), (1, 0)):
        for side in range(2):
            at, to = [
                [(samples - HALO, HALO), (samples - 2 * HALO, 0)],
                [(0, after), (HALO, after + HALO)],
            ][side][part]
            n = (part * 2 + s) * 2 + side
            halo[part, s, side] = send(
                rec_in.at[s, :, :, pl.ds(at, HALO)], ext.at[s, :, :, pl.ds(to, HALO)],
                halo_send.at[n], halo_recv.at[n], band(1 - 2 * side),
            )

    def analyse(s, first_f, number):
        blocks = [
            jnp.concatenate([ext[s, c, :, pl.ds((first_f + b) * HOP, HOP)] for c in range(comps)], axis=0)
            for b in range(number + 2 * MARGIN)
        ]
        total = None
        for tap in range(TAPS):
            term = jnp.dot(
                jnp.concatenate(blocks[tap : tap + number], axis=0),
                table[pl.ds(tap * HOP, HOP), :],
                preferred_element_type=f32,
            )
            total = term if total is None else total + term
        coef[s, pl.ds(first_f * traces, number * traces), :] = total.astype(jnp.bfloat16)

    def take_halo(part, s):
        halo[part, s, 0].wait_recv()
        halo[part, s, 1].wait_recv()
        low = (1 - part) * HALO

        @pl.when(t == 0)
        def _():
            ext[s, :, :, pl.ds(low, HALO)] = jnp.zeros((comps, rec_dev, HALO), jnp.bfloat16)

        @pl.when(t == groups - 1)
        def _():
            ext[s, :, :, pl.ds(after + part * HALO, HALO)] = jnp.zeros((comps, rec_dev, HALO), jnp.bfloat16)

    table_copy.wait()
    rec_copy.wait()
    take_halo(0, 1)
    analyse(1, MARGIN, frames)
    diagonal = lax.broadcasted_iota(i32, (traces, LANES), 0) == lax.broadcasted_iota(i32, (traces, LANES), 1)
    power = jnp.zeros((traces, LANES), f32)
    for f in range(frames):
        o = coef[1, pl.ds((MARGIN + f) * traces, traces), :].astype(f32)
        power = power + (o[:, :LANES] * o[:, :LANES] + o[:, LANES:] * o[:, LANES:])
    power = jnp.broadcast_to(jnp.sum(power, axis=1, keepdims=True), (traces, LANES))
    power = jnp.sum(jnp.where(diagonal, power, 0.0), axis=0, keepdims=True)
    lv_out[...] = jnp.broadcast_to(power, lv_out.shape)
    for d in range(1, groups):
        send(lv_out, lv_in.at[d - 1], one_send.at[1], one_recv.at[1], band(d))
    lane = lax.broadcasted_iota(i32, (rec_dev, LANES), 1)
    line = lax.broadcasted_iota(i32, (rec_dev, LANES), 0)
    listed = lane < rec_dev

    def widened(ref, n):
        across[n : n + 1, pl.ds(0, rec_dev)] = ref[n : n + 1, :]
        return jnp.broadcast_to(across[n : n + 1, :], (rec_dev, LANES))

    def upright(values):
        return jnp.broadcast_to(jnp.sum(jnp.where(line == lane, values, 0), axis=1, keepdims=True), (rec_dev, LANES))

    across[...] = jnp.zeros_like(across)
    own_t = widened(owner, 0)
    own = upright(own_t)
    first, last = upright(widened(valid, 0)), upright(widened(valid, 1))
    bins[...] = jnp.zeros_like(bins)
    bins[:, pl.ds(0, BINS)] = mask[...].astype(f32)
    before = listed & (lane < line)

    def count(what):
        return jnp.broadcast_to(jnp.sum(jnp.where(what, 1, 0), axis=1, keepdims=True), (rec_dev, LANES))

    def count_t(what):
        return jnp.broadcast_to(jnp.sum(jnp.where(what, 1, 0), axis=0, keepdims=True), (rec_dev, LANES))

    far = lax.rem(own // 2 + chips - z, chips)
    far_t = lax.rem(own_t // 2 + chips - z, chips)
    rank = count(before & (own_t == own))
    turn = count(before & (far_t == half))
    turn_t = count_t((line < lane) & (far == half))
    up = ((far > 0) & (far < half)) | ((far == half) & (turn % 2 == 0))
    up_t = ((far_t > 0) & (far_t < half)) | ((far_t == half) & (turn_t % 2 == 0))
    down = (far > half) | ((far == half) & (turn % 2 == 1))
    down_t = (far_t > half) | ((far_t == half) & (turn_t % 2 == 1))
    same = before & (far_t == far)
    place_up = count(listed & up_t & ((far_t > far) | same))
    place_down = count(listed & down_t & ((far_t < far) | same))
    place = jnp.where(up, place_up, jnp.where(down, rec_dev + place_down, line))
    key = far * (2 * MOST) + (own % 2) * MOST + rank
    sent = jnp.sum(jnp.where(key == lane, place + 1, 0), axis=0, keepdims=True)
    meta_out[...] = jnp.broadcast_to(sent, meta_out.shape)
    taken = jnp.sum(jnp.where((place == lane) & (up | down), line, 0), axis=0, keepdims=True)
    order[...] = jnp.broadcast_to(taken, order.shape)
    order_copy = pltpu.make_async_copy(order, order_s, local.at[0])
    order_copy.start()
    own_copy = pltpu.make_async_copy(meta_out, meta_s.at[0], local.at[1])
    own_copy.start()
    for d in range(1, chips):
        send(meta_out, meta_in.at[d - 1], one_send.at[0], one_recv.at[0], chip(d))

    take_halo(0, 0)
    analyse(0, MARGIN, frames)
    for s in (1, 0):
        take_halo(1, s)
        analyse(s, 0, MARGIN)
        analyse(s, MARGIN + frames, MARGIN)

    wait_bytes(lv_in, one_recv.at[1])
    power = lv_out[...]
    for d in range(1, groups):
        power = power + lv_in[d - 1]
    power = jnp.broadcast_to(power[0:1], (traces, LANES))
    power = jnp.sum(jnp.where(diagonal, power, 0.0), axis=1, keepdims=True)
    level = jnp.broadcast_to(WATER * (power / (frames * groups * BINS)) + EPSILON, (traces, LANES))

    first, last, bands = (jnp.concatenate([v] * comps, axis=0) for v in (first, last, bins[...]))
    for f in range(frames + 2 * MARGIN):
        center = (t * frames + f - MARGIN) * HOP + HOP // 2
        weight = jnp.where((first <= center) & (center < last), bands, 0.0)
        x = coef[0, pl.ds(f * traces, traces), :].astype(f32)
        y = coef[1, pl.ds(f * traces, traces), :].astype(f32)
        x_re, x_im, y_re, y_im = x[:, :LANES], x[:, LANES:], y[:, :LANES], y[:, LANES:]
        x_inv = lax.rsqrt(x_re * x_re + x_im * x_im + level)
        y_inv = lax.rsqrt(y_re * y_re + y_im * y_im + level)
        d_re = weight * (x_re * x_inv - y_re * y_inv)
        d_im = weight * (x_im * x_inv - y_im * y_inv)
        inner = (x_re * d_re + x_im * d_im) * (x_inv * x_inv * x_inv)
        adj[pl.ds(f * traces, traces), pl.ds(0, LANES)] = (d_re * x_inv - x_re * inner).astype(jnp.bfloat16)
        adj[pl.ds(f * traces, traces), pl.ds(LANES, LANES)] = (d_im * x_inv - x_im * inner).astype(jnp.bfloat16)

    for tap in range(TAPS):
        term = lax.dot_general(
            adj[pl.ds((2 * MARGIN - tap) * traces, frames * traces), :], table[pl.ds(tap * HOP, HOP), :],
            (((1,), (1,)), ((), ())), preferred_element_type=f32,
        )
        acc[...] = term if tap == 0 else acc[...] + term
    for b in range(frames):
        block = acc[pl.ds(b * traces, traces), :]
        for h in range(HOP // LANES):
            j = b * (HOP // LANES) + h
            flat[pl.ds(j * traces, traces), :] = block[:, h * LANES : (h + 1) * LANES]

    order_copy.wait()
    own_copy.wait()
    for c in range(comps):
        for r in range(rec_dev):
            row = flat[pl.ds(c * rec_dev + r, per_row, stride=traces), :]
            rows[r, pl.ds(c * per_row, per_row), :] = row.astype(jnp.bfloat16)
    flying = {}

    def hop(k, g, i):
        first_p, number, _ = parts[g]
        run = pl.ds(first_p, number)
        src = packet.at[i, run] if k == 1 else bufs[2 * (k - 2) + i].at[run]
        if k > 2:
            flying[k - 2, g, i].wait_send()
        flying[k, g, i] = send(
            src, bufs[2 * (k - 1) + i].at[run], ring_send.at[(g * 2 + k % 2) * 2 + i],
            ring_recv.at[((k - 1) * len(parts) + g) * 2 + i], chip(1 - 2 * i),
        )

    for g, (first_p, number, _) in enumerate(parts):
        for i in range(2):
            for p in range(first_p, first_p + number):
                packet[i, p] = rows[order_s[0, i * rec_dev + p]]
            hop(1, g, i)

    wait_bytes(meta_in, one_recv.at[0])
    got = pltpu.make_async_copy(meta_in, meta_s.at[pl.ds(1, chips - 1)], local.at[2])
    got.start()
    got.wait()

    whole = comps * per_row

    def keep(source, rank, row, whose):
        slot = (lax.rem(z + source + chips, chips) * 2 + whose) * MOST + rank
        slots[pl.ds(pl.multiple_of(slot * whole, whole), whole), :] = row.astype(f32)

    def deal(source, j, read):
        for e in range(2 * MOST):
            mine, rank = e // MOST == 0, e % MOST
            whose = core if mine else 1 - core
            away = (-source) % chips
            v = meta_s[away, 0, away * 2 * MOST + whose * MOST + rank]
            row = jnp.where(v > 0, read(v), jnp.zeros((), jnp.bfloat16))
            if mine:
                keep(source, rank, row, core)
            else:
                mate_out[j, rank] = row

    def from_ring(k, i):
        def read(v):
            at = jnp.clip(v - 1 - i * rec_dev, 0, hops[k - 1] - 1)
            return bufs[2 * (k - 1) + i][at]

        return read

    def from_both(v):
        return jnp.where(v > rec_dev, from_ring(half, 1)(v), from_ring(half, 0)(v))

    deal(0, 0, lambda v: rows[jnp.clip(v - 1, 0, rec_dev - 1)])
    mates = []

    def to_mate(first_j, number):
        ref = (mate_out.at[pl.ds(first_j, number)], mate_in.at[pl.ds(first_j, number)])
        mates.append((first_j, number, send(*ref, one_send.at[2], mate_recv.at[len(mates)], mate)))

    steps = sorted((k / (depth + 2), g, k) for g, (_, _, depth) in enumerate(parts) for k in range(1, depth + 1))
    waits = {k: sum(depth >= k for _, _, depth in parts) for k in range(1, half + 1)}
    ready = 1
    for _, g, k in steps:
        for i in range(2):
            flying[k, g, i].wait_recv()
            if k < parts[g][2]:
                hop(k + 1, g, i)
        waits[k] -= 1
        while ready < half and waits[ready] == 0:
            for i in range(2):
                deal(-ready if i == 0 else ready, 2 * ready - 1 + i, from_ring(ready, i))
            if ready % 2 == 1 and ready > 1:
                to_mate(*((0, 7) if ready == 3 else (2 * ready - 3, 4)))
            ready += 1
    deal(half, 2 * half - 1, from_both)
    to_mate(2 * half - 1, 1)
    source_of = [0] + [s for k in range(1, half) for s in (-k, k)] + [half]
    for first_j, number, copy in mates:
        copy.wait_recv()
        for j in range(first_j, first_j + number):
            for rank in range(MOST):
                keep(source_of[j], rank, mate_in[j, rank], 1 - core)
    kept = chips * 2 * MOST
    for c in range(comps):
        for j in range(per_row):
            part = slots[pl.ds(c * per_row + j, kept, stride=whole), :]
            out[c, :, pl.ds(j * LANES, LANES)] = part.astype(jnp.bfloat16)

    for copy in halo.values():
        copy.wait_send()
    for g, (_, _, depth) in enumerate(parts):
        for k in range(max(1, depth - 1), depth + 1):
            for i in range(2):
                flying[k, g, i].wait_send()
    wait_bytes(meta_in, one_send.at[0])
    wait_bytes(lv_in, one_send.at[1])
    wait_bytes(mate_out, one_send.at[2])


def solution(mesh):
    chips, groups = mesh.shape["space"] // 2, mesh.shape["tm"]

    def on_device(recordings, owner, valid_range, bin_mask):
        _, comps, rec_dev, samples = recordings.shape
        frames = samples // HOP
        traces, per_row = comps * rec_dev, samples // LANES
        kept = chips * 2 * MOST
        hops = ring_rows(chips, rec_dev)
        parts = len(ring_groups(hops))
        bf16, f32, i32 = jnp.bfloat16, jnp.float32, jnp.int32
        sizes = (chips, groups, comps, rec_dev, frames)
        dma = pltpu.SemaphoreType.DMA
        args = (recordings, owner.T, valid_range.T, bin_mask, jnp.asarray(cq_table()))
        args = [pltpu.with_memory_space_constraint(x, pltpu.HBM) for x in args]
        return pl.pallas_call(
            functools.partial(kernel, sizes),
            out_shape=pltpu.VMEM((comps, kept, samples), bf16),
            in_specs=[pl.BlockSpec(memory_space=space) for space in (pl.ANY, pltpu.VMEM, pltpu.VMEM, pltpu.VMEM, pl.ANY)],
            out_specs=pl.BlockSpec(memory_space=pltpu.VMEM),
            scratch_shapes=[
                pltpu.VMEM((KERNEL, 2 * LANES), bf16),
                pltpu.VMEM((rec_dev, LANES), f32),
                pltpu.VMEM((8, LANES), i32),
                pltpu.VMEM((2, comps, rec_dev, samples + 4 * HALO), bf16),
                pltpu.VMEM((2, (frames + 2 * MARGIN) * traces, 2 * LANES), bf16),
                pltpu.VMEM(((frames + 2 * MARGIN) * traces, 2 * LANES), bf16),
                pltpu.VMEM((frames * traces, HOP), f32),
                pltpu.VMEM((8, LANES), f32),
                pltpu.VMEM((groups - 1, 8, LANES), f32),
                pltpu.VMEM((8, LANES), i32),
                pltpu.VMEM((chips - 1, 8, LANES), i32),
                pltpu.VMEM((8, LANES), i32),
                pltpu.SMEM((chips, 8, LANES), i32),
                pltpu.SMEM((8, LANES), i32),
                pltpu.VMEM((per_row * traces, LANES), f32),
                pltpu.VMEM((rec_dev, comps * per_row, LANES), bf16),
                pltpu.VMEM((2, rec_dev, comps * per_row, LANES), bf16),
                pltpu.VMEM((chips, MOST, comps * per_row, LANES), bf16),
                pltpu.VMEM((chips, MOST, comps * per_row, LANES), bf16),
                pltpu.VMEM((kept * comps * per_row, LANES), f32),
                dma((8,)), dma((8,)), dma((3,)), dma((2,)),
                dma((4 * parts,)), dma((chips * parts,)), dma((chips // 4,)), dma((5,)),
            ] + [pltpu.VMEM((n, comps * per_row, LANES), bf16) for n in hops for _ in range(2)],
            compiler_params=pltpu.CompilerParams(
                collective_id=0, has_side_effects=True, vmem_limit_bytes=40 << 20
            ),
        )(*args)

    return jax.shard_map(
        on_device,
        mesh=mesh,
        in_specs=(
            P(None, None, "space", "tm"),
            P("space", None),
            P("space", None),
            P("space", None),
        ),
        out_specs=P(None, "space", "tm"),
        check_vma=False,
    )
```
